32 devices in a mesh: groups: 1, clus: 8 (over z, core), sub: 4 (over y, x).
Axes of the slice: x: 2, y: 2, z: 4, core: 2. Of those that a mesh axis runs over, the one named last changes fastest.
Arguments:
- loads: bfloat16 [12, 3, 65536], P(None, None, ('groups', 'clus', 'sub')), may hold values from -6 to 6
- centers: bfloat16 [3, 65536], P(None, ('groups', 'clus', 'sub'))
- basis: bfloat16 [256, 96, 3, 256], P(('groups', 'clus', 'sub')), may hold values from -0.625 to 0.625
- up_leaf: bfloat16 [256, 96, 96], P(('groups', 'clus', 'sub')), may hold values from -0.625 to 0.625
- up_mid: bfloat16 [128, 96, 96], P(('groups', 'clus', 'sub')), may hold values from -0.625 to 0.625
- up_top: bfloat16 [64, 96, 96], P(('groups', 'clus', 'sub')), may hold values from -0.625 to 0.625
- couplings: bfloat16 [480, 12, 96, 96], P(('groups', 'clus', 'sub')), may hold values from -0.046875 to 0.046875
- far_dest: int32 [480, 12], P(('groups', 'clus', 'sub')), may hold values from 0 to 31, all different within a row; in each aligned block of 15 rows (0 to 14, 15 to 29, ...) at most 6 rows name the same one
- far_target: int32 [480, 12], P(('groups', 'clus', 'sub')), may hold values from 0 to 7, as said below
- near_src: int32 [256, 6], P(('groups', 'clus', 'sub')), may hold values from 0 to 255, as said below
Outputs:
- field: float32 [12, 3, 65536], P(None, None, ('groups', 'clus', 'sub'))
The draws below stay inside these ranges and needn't reach their ends.
Inputs may be any that keep to these rules, and one draw needn't show every extreme that they name: `far_dest`: the rows of one device (aligned blocks of 15 rows) name one device at most 6 times in all, some device exactly so; a row names 12 different devices. far_target[r, k] is below the number of clusters a device holds at the level of row r: 8, 4, 2 or 1. `near_src`: row t starts with t; its other entries differ from t and lie at most 8 leaves from t, some exactly 8.
All inputs are finite; a program needn't handle non-finite values.
Results may differ from the reference program's by a relative error of at most 0.0095.
Values may be sent and summed in bfloat16 or wider, within the bound.
A program may use at most 64 MiB of HBM per device.

```python
import math
import jax
import jax.numpy as jnp
import numpy as np
from jax import lax

LEAF = 256
RANK3 = 96
CASES = 12
LEAF_DEV = 8
NEAR = 6
FAR_TOP = 12
DEVP = 32
CL_DEV = 15
CAP = 6
NLEAF = 256
NCL = 480
PANELS = 65536
N_CLUS = 8
N_SUB = 4


def draw_centers(key, part):
    key = jax.random.fold_in(key, 7)
    panel = jnp.arange(PANELS)
    angle = (panel // LEAF).astype(jnp.float32) * (6.2831853 / NLEAF)
    centre = jnp.stack([5.0 * jnp.cos(angle), 5.0 * jnp.sin(angle), 1.5 * jnp.sin(3.0 * angle)])
    jitter = jax.random.uniform(key, (3, PANELS), jnp.float32, -1.0, 1.0)
    return (centre + jitter).astype(jnp.bfloat16)


def draw_far_target(key, part):
    key = jax.random.fold_in(key, 5)
    rows = jnp.arange(NCL) % CL_DEV
    sizes = jnp.where(rows < LEAF_DEV, LEAF_DEV, jnp.where(rows < LEAF_DEV + LEAF_DEV // 2, LEAF_DEV // 2, jnp.where(rows < CL_DEV - 1, 2, 1)))
    return jax.random.randint(key, (NCL, FAR_TOP), 0, sizes[:, None]).astype(jnp.int32)


def draw_near_src(key, part):
    key = jax.random.fold_in(key, 11)
    rows = jnp.arange(NLEAF, dtype=jnp.int32)
    keys = jax.random.split(key, NLEAF)
    steps = jnp.concatenate([jnp.arange(-LEAF_DEV, 0), jnp.arange(1, LEAF_DEV + 1)]).astype(jnp.int32)
    picks = jax.vmap(lambda k: jax.random.permutation(k, steps)[:NEAR - 1])(keys)
    first = jnp.where(rows % LEAF_DEV == 0, LEAF_DEV, picks[:, 0])
    picks = picks.at[:, 0].set(first)
    cand = rows[:, None] + picks
    cand = jnp.where((cand < 0) | (cand >= NLEAF), rows[:, None] - picks, cand)
    return jnp.concatenate([rows[:, None], cand], axis=1).astype(jnp.int32)


def block_scale(key, extent, shards, least, largest):
    loudness = 1.0
    for position, blocks in shards:
        heights = jax.random.uniform(jax.random.fold_in(jax.random.fold_in(key, 6), position), (blocks,), jnp.float32, least / len(shards), largest / len(shards))
        loudness = loudness * jnp.repeat(jnp.exp(heights), extent[position] // blocks).reshape((-1,) + (1,) * (len(extent) - 1 - position))
    return loudness


def shared_out(rng, own, number, rows, amount, top, limit, lean):
    sequence = jax.random.permutation(rng, amount)
    heavy_load, usual = portions_of(amount, rows * top, limit, lean, True), portions_of(amount, rows * top, limit, lean, False)
    places = jnp.arange(amount)

    def named(tallies, turn):
        used = int((tallies > 0).sum())
        fixed = max(1, used // 4)
        passed = fixed + (places - fixed + turn * (used - fixed)) % max(1, amount - fixed)
        return jnp.zeros((amount,), jnp.int32).at[sequence[jnp.where(places < fixed, places, passed)]].set(jnp.asarray(tallies, jnp.int32))

    tallies = jnp.where(number % 4 == 0, named(heavy_load, number // 4), named(usual, number - number // 4 - 1))
    mixed = jax.random.permutation(jax.random.fold_in(own, 3), amount)
    source_of, receiver = mixed[0:amount // 2 * 2:2], mixed[1:amount // 2 * 2:2]
    slack = jnp.minimum(tallies[source_of] - 1, limit - tallies[receiver]) // 2
    slack = jnp.where((source_of == sequence[0]) | (receiver == sequence[0]) | (tallies[receiver] == 0), 0, jnp.maximum(slack, 0))
    passed = jax.random.randint(jax.random.fold_in(own, 4), (amount // 2,), 0, 1 << 20) % (slack + 1)
    tallies = tallies.at[source_of].add(-passed).at[receiver].add(passed)
    labels = jnp.searchsorted(jnp.cumsum(tallies), jnp.arange(rows * top), side="right").astype(jnp.int32)
    listing = labels.reshape(top, rows).T
    listing = listing[jax.random.permutation(jax.random.fold_in(own, 1), rows)]
    turn = jax.random.randint(jax.random.fold_in(own, 2), (rows, 1), 0, top)
    return jnp.take_along_axis(listing, (jnp.arange(top)[None, :] + turn) % top, axis=1)


def portions_of(number_of, total, limit, slope, full):
    weights = [(1 << 20) // math.isqrt(standing ** slope) + 1 for standing in range(1, number_of + 1)]
    largest = limit if full else min(limit, max(-(-total // number_of), total * weights[0] // sum(weights)))
    least = 1 if total - largest >= number_of - 1 else 0
    holding, surplus = [largest] + [least] * (number_of - 1), total - largest - least * (number_of - 1)
    while surplus > 0:
        free = [i for i in range(1, number_of) if holding[i] < largest] or [i for i in range(1, number_of) if holding[i] < limit]
        pool, left = sum([weights[i] for i in free]), surplus
        for i in free:
            extra = min(limit - holding[i], max(1, left * weights[i] // pool), surplus)
            holding[i] = holding[i] + extra
            surplus = surplus - extra
    return np.array(holding)


def scatter_about(key, extent, scale, limit, cuts=(), held_as=jnp.bfloat16):
    result = scale * jax.random.normal(key, extent, jnp.float32)
    if cuts:
        result = result * block_scale(key, extent, cuts, -0.22, 0.18)
    return jnp.clip(result, -limit, limit).astype(held_as)


def setup_inputs(seed: int = 0, part: int = 0) -> dict:
    arg_keys = jax.random.split(jax.random.key(seed), 11)
    part_splits = jax.random.split(jax.random.fold_in(arg_keys[10], part), 11)
    loads = scatter_about(part_splits[0], (CASES, 3, PANELS), 1.0, 6.0, ((2, 32),))
    centers = draw_centers(jax.random.fold_in(jax.random.fold_in(arg_keys[10], part), 71), part)
    basis = scatter_about(part_splits[2], (NLEAF, RANK3, 3, LEAF), RANK3 ** -0.5, 0.625, ((0, 32),))
    up_leaf = scatter_about(part_splits[3], (NLEAF, RANK3, RANK3), RANK3 ** -0.5, 0.625, ((0, 32),))
    up_mid = scatter_about(part_splits[4], (NLEAF // 2, RANK3, RANK3), RANK3 ** -0.5, 0.625, ((0, 32),))
    up_top = scatter_about(part_splits[5], (NLEAF // 4, RANK3, RANK3), RANK3 ** -0.5, 0.625, ((0, 32),))
    couplings = scatter_about(part_splits[6], (NCL, FAR_TOP, RANK3, RANK3), (RANK3 * FAR_TOP * 16) ** -0.5, 0.046875, ((0, 32),))
    far_dest_keys = jax.random.split(jax.random.fold_in(part_splits[7], 1), NCL // CL_DEV)
    far_dest_turns = jax.random.permutation(jax.random.fold_in(part_splits[7], 3), NCL // CL_DEV)
    far_dest = jax.vmap(lambda own, number: shared_out(jax.random.fold_in(part_splits[7], 2), own, number, CL_DEV, DEVP, FAR_TOP, CAP, 2))(far_dest_keys, far_dest_turns).reshape((NCL, FAR_TOP))
    far_target = draw_far_target(jax.random.fold_in(jax.random.fold_in(arg_keys[10], part), 71), part)
    near_src = draw_near_src(jax.random.fold_in(jax.random.fold_in(arg_keys[10], part), 71), part)
    return dict(loads=loads, centers=centers, basis=basis, up_leaf=up_leaf, up_mid=up_mid, up_top=up_top, couplings=couplings, far_dest=far_dest, far_target=far_target, near_src=near_src)


CORE_SQ = 0.0625
KELVIN = 1.0 / (16.0 * math.pi * 0.7)
SHEAR = 1.8

def kelvin_tile(target_pts, source_pts):
    diff = target_pts[None, :, :, None] - source_pts[:, :, None, :]
    dist_sq = lax.optimization_barrier(jnp.sum(diff * diff, axis=1)) + CORE_SQ
    scale = KELVIN * lax.rsqrt(dist_sq)
    inverse = 1.0 / dist_sq
    outer = diff[:, :, None] * diff[:, None, :] * inverse[:, None, None]
    eye_block = jnp.eye(3, dtype=jnp.float32)[None, :, :, None, None]
    return ((SHEAR * eye_block + outer) * scale[:, None, None]).astype(jnp.bfloat16)

def climb(weights, child):
    prod = jnp.einsum('kab,kbc->kac', weights.astype(jnp.float32), child.astype(jnp.float32))
    prod = prod.reshape(prod.shape[0] // 2, 2, prod.shape[1], prod.shape[2])
    return (prod[:, 0] + prod[:, 1]).astype(jnp.bfloat16)

def descend(weights, incoming, parent):
    spread = jnp.repeat(parent, 2, axis=0)
    moved = jnp.einsum('kab,kac->kbc', weights.astype(jnp.float32), spread.astype(jnp.float32))
    return (incoming + moved).astype(jnp.bfloat16)

def level_offsets(per_dev):
    sizes = [per_dev, per_dev // 2, per_dev // 4, per_dev // 8]
    starts = [0, per_dev, per_dev + per_dev // 2, per_dev + per_dev // 2 + per_dev // 4]
    return np.concatenate([np.full(sizes[k], starts[k]) for k in range(4)]).astype(np.int32)

def reference(loads, centers, basis, up_leaf, up_mid, up_top, couplings, far_dest, far_target, near_src):
    ndev = N_CLUS * N_SUB
    nleaf, rank3, _, leaf = basis.shape
    cases = loads.shape[0]
    per_dev = nleaf // ndev
    blocks = loads.reshape(cases, 3, nleaf, leaf)
    coef_leaf = jnp.einsum('trip,citp->trc', basis.astype(jnp.float32), blocks.astype(jnp.float32)).astype(jnp.bfloat16)
    coef_mid = climb(up_leaf, coef_leaf)
    coef_high = climb(up_mid, coef_mid)
    coef_top = climb(up_top, coef_high)
    levels = [coef_leaf, coef_mid, coef_high, coef_top]
    coef_all = jnp.concatenate([lv.reshape(ndev, -1, rank3, cases) for lv in levels], axis=1)
    per_row = coef_all.shape[1]

    def device_terms(index):
        mats = couplings.reshape(ndev, per_row, -1, rank3, rank3)[index]
        prod = jnp.einsum('rkab,rbc->rkac', mats.astype(jnp.float32), coef_all[index].astype(jnp.float32))
        return prod.astype(jnp.bfloat16)
    contrib = lax.map(device_terms, jnp.arange(ndev, dtype=jnp.int32))
    offsets = jnp.asarray(np.tile(level_offsets(per_dev), ndev), dtype=jnp.int32)
    target = far_dest * per_row + offsets[:, None] + far_target
    incoming = jax.ops.segment_sum(contrib.reshape(-1, rank3, cases).astype(jnp.float32), target.reshape(-1), num_segments=ndev * per_row)
    incoming = incoming.reshape(ndev, per_row, rank3, cases)
    lo1 = per_dev
    lo2 = lo1 + per_dev // 2
    lo3 = lo2 + per_dev // 4
    inc_leaf = incoming[:, :lo1].reshape(-1, rank3, cases)
    inc_mid = incoming[:, lo1:lo2].reshape(-1, rank3, cases)
    inc_high = incoming[:, lo2:lo3].reshape(-1, rank3, cases)
    w_top = incoming[:, lo3:].reshape(-1, rank3, cases).astype(jnp.bfloat16)
    w_high = descend(up_top, inc_high, w_top)
    w_mid = descend(up_mid, inc_mid, w_high)
    w_leaf = descend(up_leaf, inc_leaf, w_mid)
    far = jnp.einsum('trip,trc->citp', basis.astype(jnp.float32), w_leaf.astype(jnp.float32))
    pts = centers.astype(jnp.float32).reshape(3, nleaf, leaf)

    def one_leaf(index):
        srcs = near_src[index]
        src_pts = jnp.transpose(pts[:, srcs], (1, 0, 2))
        tile = kelvin_tile(pts[:, index], src_pts)
        src_loads = blocks[:, :, srcs]
        return jnp.einsum('kijpq,cjkq->cip', tile.astype(jnp.float32), src_loads.astype(jnp.float32))
    near = lax.map(one_leaf, jnp.arange(nleaf, dtype=jnp.int32))
    near = jnp.transpose(near, (1, 2, 0, 3))
    return (far + near).reshape(cases, 3, nleaf * leaf)
```

```python
import functools
import math

import jax
import jax.numpy as jnp
from jax import lax
from jax.experimental import pallas as pl
from jax.experimental.pallas import tpu as pltpu
from jax.sharding import PartitionSpec as P

CORE_SQ = 0.0625
KELVIN = 1.0 / (16.0 * math.pi * 0.7)
SHEAR = 1.8
F32 = jnp.float32
BF16 = jnp.bfloat16
NT = (((1,), (1,)), ((), ()))
CH = 32


def dot_nt(a, b):
    return lax.dot_general(a, b, NT, preferred_element_type=F32)


def dot(a, b):
    return jnp.dot(a, b, preferred_element_type=F32)


def kernel(dims, pack, basis, up_leaf, up_mid, up_top, coup, dest, target, near_src, out,
           win, bas_v, ul_v, um_v, ut_v, coup_v, coef, labels, tab_v, tab, send, got,
           lhs, ycol, tiles, near, inc, w, in_sem, halo_send, halo_recv, a2a_send, a2a_recv):
    ndev, nsub, cap, nl, fan, rank, leaf = dims
    rows = cap * 16
    per_row = 2 * nl - 1
    nb = per_row * fan
    nbp = (nb + 15) // 16 * 16
    lin = lax.axis_index("clus") * nsub + lax.axis_index("sub")

    def place(index):
        return {"clus": index // nsub, "sub": lax.rem(index, nsub)}

    barrier = pltpu.get_barrier_semaphore()

    def greet(step, carry):
        other = lax.rem(lin + step, ndev)
        pl.semaphore_signal(barrier, inc=1, device_id=place(other), device_id_type=pl.DeviceIdType.MESH)
        return carry

    loads_in = [
        pltpu.make_async_copy(pack, win.at[1], in_sem.at[0]),
        pltpu.make_async_copy(basis, bas_v, in_sem.at[1]),
        pltpu.make_async_copy(up_leaf, ul_v, in_sem.at[2]),
        pltpu.make_async_copy(up_mid, um_v, in_sem.at[3]),
        pltpu.make_async_copy(up_top, ut_v, in_sem.at[4]),
        pltpu.make_async_copy(coup, coup_v, in_sem.at[5]),
    ]
    for copy in loads_in:
        copy.start()
    lax.fori_loop(1, ndev, greet, 0)

    row_i = lax.broadcasted_iota(jnp.int32, (per_row, fan), 0)
    off = jnp.where(row_i < nl, 0, jnp.where(row_i < nl + nl // 2, nl, jnp.where(row_i < per_row - 1, nl + nl // 2, per_row - 1)))
    goal = ((target[...] + off) * 16).astype(F32)
    dst = dest[...].astype(F32)
    b_row = lax.broadcasted_iota(jnp.int32, (nbp, per_row), 0) // fan
    pick_r = (b_row == lax.broadcasted_iota(jnp.int32, (nbp, per_row), 1)).astype(F32)
    b_fan = lax.rem(lax.broadcasted_iota(jnp.int32, (nbp, fan), 0), fan)
    pick_k = b_fan == lax.broadcasted_iota(jnp.int32, (nbp, fan), 1)
    valid = lax.broadcasted_iota(jnp.int32, (nbp, 1), 0) < nb

    def column(values):
        spread = dot(pick_r.astype(BF16), values.astype(BF16))
        return jnp.sum(jnp.where(pick_k, spread, 0.0), axis=1, keepdims=True)

    dest_c = jnp.where(valid, column(dst), -1.0)
    goal_c = column(goal)
    sub_b = lax.broadcasted_iota(jnp.int32, (nbp, nbp), 0)
    lane_b = lax.broadcasted_iota(jnp.int32, (nbp, nbp), 1)
    dest_r = jnp.sum(jnp.where(sub_b == lane_b, dest_c, 0.0), axis=0, keepdims=True)
    rank_c = jnp.sum(jnp.where((dest_c == dest_r) & (lane_b < sub_b), 1.0, 0.0), axis=1, keepdims=True)
    lane = lax.broadcasted_iota(jnp.int32, (nbp, 128), 1)
    number = lax.broadcasted_iota(jnp.int32, (nbp, 128), 0).astype(F32)
    slot_of = (lane // 16).astype(F32)
    hits = rank_c == slot_of
    tag_w = jnp.where(hits & (lane < rows), goal_c + 1.0, 0.0).astype(BF16)
    num_w = jnp.where(rank_c == lane.astype(F32), number, 0.0).astype(BF16)
    who = lax.broadcasted_iota(jnp.int32, (ndev, nbp), 0).astype(F32)
    mine = (who == dest_r).astype(F32).astype(BF16)
    tags = dot(mine, tag_w)
    lane_d = lax.broadcasted_iota(jnp.int32, (ndev, 128), 1)
    comp = lax.rem(lane_d, 16)
    labels[...] = jnp.where((tags > 0.5) & (comp < 12), tags - 1.0 + comp.astype(F32), 255.0)
    tab_v[...] = dot(mine, num_w).astype(jnp.int32)
    to_smem = pltpu.make_async_copy(tab_v, tab, in_sem.at[6])
    to_smem.start()

    loads_in[0].wait()
    loads_in[1].wait()
    for t in range(nl):
        total = jnp.zeros((16, rank), F32)
        for i in range(3):
            total += dot_nt(win[1, i, :, t * leaf:(t + 1) * leaf], bas_v[t, i])
        coef[t] = total.astype(BF16)
    for copy in loads_in[2:5]:
        copy.wait()
    lower, upper = 0, nl
    for mats, count in ((ul_v, nl), (um_v, nl // 2), (ut_v, nl // 4)):
        for k in range(count // 2):
            total = dot_nt(coef[lower + 2 * k], mats[2 * k]) + dot_nt(coef[lower + 2 * k + 1], mats[2 * k + 1])
            coef[upper + k] = total.astype(BF16)
        lower, upper = upper, upper + count // 2

    pl.semaphore_wait(barrier, ndev - 1)
    right = lax.rem(lin + 1, ndev)
    left = lax.rem(lin + ndev - 1, ndev)
    to_right = pltpu.make_async_remote_copy(
        src_ref=win.at[1], dst_ref=win.at[0], send_sem=halo_send.at[0], recv_sem=halo_recv.at[0],
        device_id=place(right), device_id_type=pl.DeviceIdType.MESH)
    to_left = pltpu.make_async_remote_copy(
        src_ref=win.at[1], dst_ref=win.at[2], send_sem=halo_send.at[1], recv_sem=halo_recv.at[1],
        device_id=place(left), device_id_type=pl.DeviceIdType.MESH)
    to_right.start()
    to_left.start()

    to_smem.wait()
    loads_in[5].wait()
    mark = lax.broadcasted_iota(jnp.int32, (16, rank), 0) == 12

    def make_block(other, store):
        for s in range(cap):
            b = jnp.clip(tab[other, s], 0, nb - 1)
            prod = dot_nt(coef[lax.div(b, fan)], coup_v[b])
            if s == 0:
                prod = jnp.where(mark, labels[pl.ds(other, 1), :rank], prod)
            store(s, prod.astype(BF16))

    def far_copy(step):
        other = lax.rem(lin + step, ndev)
        return pltpu.make_async_remote_copy(
            src_ref=send.at[step], dst_ref=got.at[step], send_sem=a2a_send.at[step], recv_sem=a2a_recv.at[step],
            device_id=place(other), device_id_type=pl.DeviceIdType.MESH)

    def couple(step, carry):
        def store(s, value):
            send[step, s * 16:(s + 1) * 16] = value
        make_block(lax.rem(lin + step, ndev), store)
        far_copy(step).start()
        return carry

    lax.fori_loop(1, ndev, couple, 0)

    def store_own(s, value):
        got[0, s * 16:(s + 1) * 16] = value
    make_block(lin, store_own)

    to_right.wait()
    to_left.wait()
    for part in range(3):
        def prepare(t, carry):
            cols = pl.ds(pl.multiple_of(t * leaf, leaf), leaf)
            cen = win[part, 3, :, cols].astype(F32)
            ycol[part * nl + t] = cen.T
            for j in range(3):
                f = win[part, j, :, cols]
                lhs[part * nl + t, j, 0:16] = f
                f32 = f.astype(F32)
                for i in range(3):
                    prod = f32 * cen[i:i + 1]
                    high = prod.astype(BF16)
                    lhs[part * nl + t, j, 16 + 16 * i:32 + 16 * i] = high
                    lhs[part * nl + t, j, 64 + 16 * i:80 + 16 * i] = (prod - high.astype(F32)).astype(BF16)
            return carry
        lax.fori_loop(0, nl, prepare, 0)

    base = lin * nl - nl
    n_near = near_src.shape[1]

    def near_leaf(t, carry):
        cols = pl.ds(pl.multiple_of(t * leaf, leaf), leaf)
        own = win[1, 3, :, cols].astype(F32)
        x = [own[i:i + 1] for i in range(3)]
        acc = jnp.zeros((112, leaf), F32)
        acc_r = [jnp.zeros((16, leaf), F32) for _ in range(3)]
        for k in range(n_near):
            s = jnp.clip(near_src[t, k] - base, 0, 3 * nl - 1)
            for c in range(leaf // CH):
                y = ycol[s, c * CH:(c + 1) * CH, :]
                v = [x[i] - y[:, i:i + 1] for i in range(3)]
                r = lax.rsqrt(v[0] * v[0] + v[1] * v[1] + v[2] * v[2] + CORE_SQ)
                kr = r * KELVIN
                rr = r * r
                tiles[k % 2, 3, c * CH:(c + 1) * CH] = (kr * SHEAR).astype(BF16)
                for j in range(3):
                    tiles[k % 2, j, c * CH:(c + 1) * CH] = ((v[j] * rr) * kr).astype(BF16)
            for j in range(3):
                acc += dot(lhs[s, j], tiles[k % 2, j])
                acc_r[j] += dot(lhs[s, j, 0:16], tiles[k % 2, 3])
        for i in range(3):
            part = acc[0:16] * x[i] - (acc[16 + 16 * i:32 + 16 * i] + acc[64 + 16 * i:80 + 16 * i])
            near[i, :, cols] = acc_r[i] + part
        return carry

    lax.fori_loop(0, nl, near_leaf, 0)

    inc[...] = jnp.zeros_like(inc)
    q_row = lax.broadcasted_iota(jnp.int32, (per_row * 16, rows), 0).astype(F32)

    def add_block(step):
        tag = got[step, 0:16, :rows].astype(F32)[12:13]
        pick = jnp.where(q_row == tag, 1.0, 0.0).astype(BF16)
        inc[...] += dot(pick, got[step])

    add_block(0)

    def collect(step, carry):
        far_copy(step).wait()
        add_block(step)
        return carry

    lax.fori_loop(1, ndev, collect, 0)

    w[per_row - 1] = inc[(per_row - 1) * 16:per_row * 16].astype(BF16)
    upper = per_row - 1
    for mats, count in ((ut_v, nl // 4), (um_v, nl // 2), (ul_v, nl)):
        lower = upper - count
        for k in range(count):
            q = lower + k
            w[q] = (inc[q * 16:(q + 1) * 16] + dot(w[upper + k // 2], mats[k])).astype(BF16)
        upper = lower
    for t in range(nl):
        for i in range(3):
            out[i, :, t * leaf:(t + 1) * leaf] = near[i, :, t * leaf:(t + 1) * leaf] + dot(w[t], bas_v[t, i])


def body(loads, centers, basis, up_leaf, up_mid, up_top, couplings, far_dest, far_target, near_src):
    cases = loads.shape[0]
    nl, rank, _, leaf = basis.shape
    nsub = lax.axis_size("sub")
    ndev = lax.axis_size("clus") * nsub
    per_row, fan = far_dest.shape
    cap = max(2, (per_row * fan + ndev - 1) // ndev)
    rows = cap * 16
    width = nl * leaf
    pack = jnp.concatenate([
        jnp.pad(jnp.transpose(loads, (1, 0, 2)), ((0, 0), (0, 16 - cases), (0, 0))),
        jnp.pad(centers[None], ((0, 0), (0, 13), (0, 0))),
    ], axis=0)
    dims = (ndev, nsub, cap, nl, fan, rank, leaf)
    hbm = pl.BlockSpec(memory_space=pl.ANY)
    vmem = pl.BlockSpec(memory_space=pltpu.VMEM)
    smem = pl.BlockSpec(memory_space=pltpu.SMEM)
    out = pl.pallas_call(
        functools.partial(kernel, dims),
        out_shape=jax.ShapeDtypeStruct((3, 16, width), F32),
        in_specs=[hbm] * 6 + [vmem, vmem, smem],
        out_specs=vmem,
        scratch_shapes=[
            pltpu.VMEM((3, 4, 16, width), BF16),
            pltpu.VMEM((nl, 3, rank, leaf), BF16),
            pltpu.VMEM((nl, rank, rank), BF16),
            pltpu.VMEM((nl // 2, rank, rank), BF16),
            pltpu.VMEM((nl // 4, rank, rank), BF16),
            pltpu.VMEM((per_row * fan, rank, rank), BF16),
            pltpu.VMEM((per_row, 16, rank), BF16),
            pltpu.VMEM((ndev, 128), F32),
            pltpu.VMEM((ndev, 128), jnp.int32),
            pltpu.SMEM((ndev, 128), jnp.int32),
            pltpu.VMEM((ndev, rows, rank), BF16),
            pltpu.VMEM((ndev, rows, rank), BF16),
            pltpu.VMEM((3 * nl, 3, 112, leaf), BF16),
            pltpu.VMEM((3 * nl, leaf, 16), F32),
            pltpu.VMEM((2, 4, leaf, leaf), BF16),
            pltpu.VMEM((3, 16, width), F32),
            pltpu.VMEM((per_row * 16, rank), F32),
            pltpu.VMEM((per_row, 16, rank), BF16),
            pltpu.SemaphoreType.DMA((7,)),
            pltpu.SemaphoreType.DMA((2,)),
            pltpu.SemaphoreType.DMA((2,)),
            pltpu.SemaphoreType.DMA((ndev,)),
            pltpu.SemaphoreType.DMA((ndev,)),
        ],
        compiler_params=pltpu.CompilerParams(
            collective_id=0, has_side_effects=True, vmem_limit_bytes=50 * 1024 * 1024
        ),
    )(pack, jnp.transpose(basis, (0, 2, 1, 3)), up_leaf, up_mid, up_top,
      couplings.reshape(per_row * fan, rank, rank), far_dest, far_target, near_src)
    return jnp.transpose(out[:, :cases], (1, 0, 2))


def solution(mesh):
    every = ("groups", "clus", "sub")
    return jax.shard_map(
        body,
        mesh=mesh,
        in_specs=(
            P(None, None, every),
            P(None, every),
            P(every, None, None, None),
            P(every, None, None),
            P(every, None, None),
            P(every, None, None),
            P(every, None, None, None),
            P(every, None),
            P(every, None),
            P(every, None),
        ),
        out_specs=P(None, None, every),
        check_vma=False,
    )
```

```python
import functools
import math

import jax
import jax.numpy as jnp
from jax import lax
from jax.experimental import pallas as pl
from jax.experimental.pallas import tpu as pltpu
from jax.sharding import PartitionSpec as P

CORE_SQ = 0.0625
KELVIN = 1.0 / (16.0 * math.pi * 0.7)
SHEAR = 1.8
F32 = jnp.float32
BF16 = jnp.bfloat16
NT = (((1,), (1,)), ((), ()))
CH = 32


def dot_nt(a, b):
    return lax.dot_general(a, b, NT, preferred_element_type=F32)


def dot(a, b):
    return jnp.dot(a, b, preferred_element_type=F32)


def kernel(dims, pack, basis, up_leaf, up_mid, up_top, coup, dest_h, target_h, near_h, out,
           dest, target, near_src, win, bas_v, ul_v, um_v, ut_v, coup_v, coef, labels, tab_v, tab, send, got,
           lhs, lhs_r, ycol, tiles, near, inc, w, in_sem, halo_send, halo_recv, a2a_send, a2a_recv):
    ndev, nsub, cap, nl, fan, rank, leaf = dims
    used = cap * 12
    rows = (used + 16) // 16 * 16
    per_row = 2 * nl - 1
    nb = per_row * fan
    nbp = (nb + 15) // 16 * 16
    lin = lax.axis_index("clus") * nsub + lax.axis_index("sub")

    def place(index):
        return {"clus": index // nsub, "sub": lax.rem(index, nsub)}

    barrier = pltpu.get_barrier_semaphore()

    def greet(step, carry):
        other = lax.rem(lin + step, ndev)
        pl.semaphore_signal(barrier, inc=1, device_id=place(other), device_id_type=pl.DeviceIdType.MESH)
        return carry

    loads_in = [
        pltpu.make_async_copy(pack, win.at[1], in_sem.at[0]),
        pltpu.make_async_copy(basis, bas_v, in_sem.at[1]),
        pltpu.make_async_copy(up_leaf, ul_v, in_sem.at[2]),
        pltpu.make_async_copy(up_mid, um_v, in_sem.at[3]),
        pltpu.make_async_copy(up_top, ut_v, in_sem.at[4]),
        pltpu.make_async_copy(coup, coup_v, in_sem.at[5]),
        pltpu.make_async_copy(dest_h, dest, in_sem.at[7]),
        pltpu.make_async_copy(target_h, target, in_sem.at[8]),
        pltpu.make_async_copy(near_h, near_src, in_sem.at[9]),
    ]
    lax.fori_loop(1, ndev, greet, 0)
    for index in (0, 6, 7, 1, 2, 3, 4, 8, 5):
        loads_in[index].start()

    loads_in[0].wait()
    pl.semaphore_wait(barrier, ndev - 1)
    right = lax.rem(lin + 1, ndev)
    left = lax.rem(lin + ndev - 1, ndev)
    to_right = pltpu.make_async_remote_copy(
        src_ref=win.at[1], dst_ref=win.at[0], send_sem=halo_send.at[0], recv_sem=halo_recv.at[0],
        device_id=place(right), device_id_type=pl.DeviceIdType.MESH)
    to_left = pltpu.make_async_remote_copy(
        src_ref=win.at[1], dst_ref=win.at[2], send_sem=halo_send.at[1], recv_sem=halo_recv.at[1],
        device_id=place(left), device_id_type=pl.DeviceIdType.MESH)
    to_right.start()
    to_left.start()

    loads_in[6].wait()
    loads_in[7].wait()
    row_i = lax.broadcasted_iota(jnp.int32, (per_row, fan), 0)
    off = jnp.where(row_i < nl, 0, jnp.where(row_i < nl + nl // 2, nl, jnp.where(row_i < per_row - 1, nl + nl // 2, per_row - 1)))
    goal = ((target[...] + off) * 16).astype(F32)
    dst = dest[...].astype(F32)
    b_row = lax.broadcasted_iota(jnp.int32, (nbp, per_row), 0) // fan
    pick_r = (b_row == lax.broadcasted_iota(jnp.int32, (nbp, per_row), 1)).astype(F32)
    b_fan = lax.rem(lax.broadcasted_iota(jnp.int32, (nbp, fan), 0), fan)
    pick_k = b_fan == lax.broadcasted_iota(jnp.int32, (nbp, fan), 1)
    valid = lax.broadcasted_iota(jnp.int32, (nbp, 1), 0) < nb

    def column(values):
        spread = dot(pick_r.astype(BF16), values.astype(BF16))
        return jnp.sum(jnp.where(pick_k, spread, 0.0), axis=1, keepdims=True)

    dest_c = jnp.where(valid, column(dst), -1.0)
    goal_c = column(goal)
    sub_b = lax.broadcasted_iota(jnp.int32, (nbp, nbp), 0)
    lane_b = lax.broadcasted_iota(jnp.int32, (nbp, nbp), 1)
    dest_r = jnp.sum(jnp.where(sub_b == lane_b, dest_c, 0.0), axis=0, keepdims=True)
    rank_c = jnp.sum(jnp.where((dest_c == dest_r) & (lane_b < sub_b), 1.0, 0.0), axis=1, keepdims=True)
    lane = lax.broadcasted_iota(jnp.int32, (nbp, 128), 1)
    number = lax.broadcasted_iota(jnp.int32, (nbp, 128), 0).astype(F32)
    slot_of = (lane // 12).astype(F32)
    hits = rank_c == slot_of
    tag_w = jnp.where(hits & (lane < used), goal_c + 1.0, 0.0).astype(BF16)
    num_w = jnp.where(rank_c == lane.astype(F32), number, 0.0).astype(BF16)
    who = lax.broadcasted_iota(jnp.int32, (ndev, nbp), 0).astype(F32)
    mine = (who == dest_r).astype(F32).astype(BF16)
    tags = dot(mine, tag_w)
    lane_d = lax.broadcasted_iota(jnp.int32, (ndev, 128), 1)
    comp = lax.rem(lane_d, 12)
    labels[...] = jnp.where(tags > 0.5, tags - 1.0 + comp.astype(F32), 255.0)
    tab_v[...] = dot(mine, num_w).astype(jnp.int32)
    to_smem = pltpu.make_async_copy(tab_v, tab, in_sem.at[6])
    to_smem.start()

    def cut(part, start, i):
        block = win[part, :, pl.ds(start, leaf)].astype(F32)
        return block[12 * i:12 * i + 16].astype(BF16)

    loads_in[1].wait()
    for t in range(nl):
        total = jnp.zeros((16, rank), F32)
        for i in range(3):
            total += dot_nt(cut(1, t * leaf, i), bas_v[t, i])
        coef[t] = total.astype(BF16)
    for copy in loads_in[2:5]:
        copy.wait()
    lower, upper = 0, nl
    for mats, count in ((ul_v, nl), (um_v, nl // 2), (ut_v, nl // 4)):
        for k in range(count // 2):
            total = dot_nt(coef[lower + 2 * k], mats[2 * k]) + dot_nt(coef[lower + 2 * k + 1], mats[2 * k + 1])
            coef[upper + k] = total.astype(BF16)
        lower, upper = upper, upper + count // 2

    to_smem.wait()
    loads_in[5].wait()
    def make_block(other):
        prods = []
        for s in range(cap):
            b = jnp.clip(tab[other, s], 0, nb - 1)
            prods.append(dot_nt(coef[lax.div(b, fan)], coup_v[b])[:12])
        prods.append(labels[pl.ds(other, 1), :rank])
        prods.append(jnp.zeros((rows - used - 1, rank), F32))
        return jnp.concatenate(prods, axis=0).astype(BF16)

    def far_copy(step):
        other = lax.rem(lin + step, ndev)
        return pltpu.make_async_remote_copy(
            src_ref=send.at[step], dst_ref=got.at[step], send_sem=a2a_send.at[step], recv_sem=a2a_recv.at[step],
            device_id=place(other), device_id_type=pl.DeviceIdType.MESH)

    def couple(group, carry):
        blocks = [make_block(lax.rem(lin + group * 4 + u, ndev)) for u in range(4)]
        for u in range(4):
            send[group * 4 + u] = blocks[u]
        for u in range(4):
            far_copy(group * 4 + u).start()
        return carry

    blocks = [make_block(lax.rem(lin + u, ndev)) for u in range(4)]
    got[0] = blocks[0]
    for u in range(1, 4):
        send[u] = blocks[u]
    for u in range(1, 4):
        far_copy(u).start()
    lax.fori_loop(1, ndev // 4, couple, 0)

    for part in (1, 0, 2):
        if part == 0:
            to_right.wait()
            to_left.wait()

        def prepare(t, carry):
            block = win[part, :, pl.ds(pl.multiple_of(t * leaf, leaf), leaf)].astype(F32)
            ycol[part * nl + t] = block[32:48].T
            for j in range(3):
                f = block[12 * j:12 * j + 16]
                lhs[part * nl + t, j, 0:16] = f.astype(BF16)
                lhs_r[part * nl + t, 16 * j:16 * j + 16] = f.astype(BF16)
                for i in range(3):
                    prod = f * block[36 + i:37 + i]
                    high = prod.astype(BF16)
                    lhs[part * nl + t, j, 16 + 16 * i:32 + 16 * i] = high
                    lhs[part * nl + t, j, 64 + 16 * i:80 + 16 * i] = (prod - high.astype(F32)).astype(BF16)
            return carry
        lax.fori_loop(0, nl, prepare, 0)

    loads_in[8].wait()
    base = lin * nl - nl
    n_near = near_src.shape[1]

    def near_leaf(t, carry):
        cols = pl.ds(pl.multiple_of(t * leaf, leaf), leaf)
        own = win[1, 32:48, cols].astype(F32)
        x = [own[4 + i:5 + i] for i in range(3)]
        acc = jnp.zeros((112, leaf), F32)
        acc_r = jnp.zeros((48, leaf), F32)
        srcs = [jnp.clip(near_src[t, k] - base, 0, 3 * nl - 1) for k in range(n_near)]
        chunks = leaf // CH
        for k in range(n_near + 1):
            for c in range(chunks):
                if k < n_near:
                    y = ycol[srcs[k], c * CH:(c + 1) * CH, :]
                    v = [x[i] - y[:, 4 + i:5 + i] for i in range(3)]
                    r = lax.rsqrt(v[0] * v[0] + v[1] * v[1] + v[2] * v[2] + CORE_SQ)
                    rr = r * r
                    tiles[k % 2, 3, c * CH:(c + 1) * CH] = r.astype(BF16)
                    for j in range(3):
                        tiles[k % 2, j, c * CH:(c + 1) * CH] = ((v[j] * rr) * r).astype(BF16)
                if k > 0 and c % (chunks // 4) == 0:
                    j = c // (chunks // 4)
                    if j < 3:
                        acc += dot(lhs[srcs[k - 1], j], tiles[(k - 1) % 2, j])
                    else:
                        acc_r += dot(lhs_r[srcs[k - 1]], tiles[(k - 1) % 2, 3])
        for i in range(3):
            part = acc[0:16] * x[i] - (acc[16 + 16 * i:32 + 16 * i] + acc[64 + 16 * i:80 + 16 * i])
            near[i, :, cols] = (acc_r[16 * i:16 * i + 16] * SHEAR + part) * KELVIN
        return carry

    lax.fori_loop(0, nl, near_leaf, 0)

    q_row = lax.broadcasted_iota(jnp.int32, (per_row * 16, rows), 0).astype(F32)

    def sum_of(group):
        total = jnp.zeros((per_row * 16, rank), F32)
        for u in range(4):
            block = got[group * 4 + u]
            tag = block[used // 16 * 16:].astype(F32)[used % 16:used % 16 + 1, :rows]
            pick = jnp.where(q_row == tag, 1.0, 0.0).astype(BF16)
            total += dot(pick, block)
        return total

    for u in range(1, 4):
        far_copy(u).wait()
    inc[...] = sum_of(0)

    def collect(group, carry):
        for u in range(4):
            far_copy(group * 4 + u).wait()
        inc[...] += sum_of(group)
        return carry

    lax.fori_loop(1, ndev // 4, collect, 0)

    w[per_row - 1] = inc[(per_row - 1) * 16:per_row * 16].astype(BF16)
    upper = per_row - 1
    for mats, count in ((ut_v, nl // 4), (um_v, nl // 2), (ul_v, nl)):
        lower = upper - count
        for k in range(count):
            q = lower + k
            w[q] = (inc[q * 16:(q + 1) * 16] + dot(w[upper + k // 2], mats[k])).astype(BF16)
        upper = lower
    for t in range(nl):
        for i in range(3):
            out[i, :, t * leaf:(t + 1) * leaf] = near[i, :, t * leaf:(t + 1) * leaf] + dot(w[t], bas_v[t, i])


def body(loads, centers, basis, up_leaf, up_mid, up_top, couplings, far_dest, far_target, near_src):
    cases = loads.shape[0]
    nl, rank, _, leaf = basis.shape
    nsub = lax.axis_size("sub")
    ndev = lax.axis_size("clus") * nsub
    per_row, fan = far_dest.shape
    cap = max(2, (per_row * fan + ndev - 1) // ndev)
    rows = (cap * 12 + 16) // 16 * 16
    width = nl * leaf
    pack = jnp.concatenate([
        jnp.transpose(loads, (1, 0, 2)).reshape(3 * cases, width), centers, jnp.zeros((9, width), BF16)
    ], axis=0)
    dims = (ndev, nsub, cap, nl, fan, rank, leaf)
    hbm = pl.BlockSpec(memory_space=pltpu.HBM)
    vmem = pl.BlockSpec(memory_space=pltpu.VMEM)
    out = pl.pallas_call(
        functools.partial(kernel, dims),
        out_shape=jax.ShapeDtypeStruct((3, 16, width), F32),
        in_specs=[hbm] * 9,
        out_specs=vmem,
        scratch_shapes=[
            pltpu.VMEM(far_dest.shape, jnp.int32),
            pltpu.VMEM(far_target.shape, jnp.int32),
            pltpu.SMEM(near_src.shape, jnp.int32),
            pltpu.VMEM((3, 48, width), BF16),
            pltpu.VMEM((nl, 3, rank, leaf), BF16),
            pltpu.VMEM((nl, rank, rank), BF16),
            pltpu.VMEM((nl // 2, rank, rank), BF16),
            pltpu.VMEM((nl // 4, rank, rank), BF16),
            pltpu.VMEM((per_row * fan, rank, rank), BF16),
            pltpu.VMEM((per_row, 16, rank), BF16),
            pltpu.VMEM((ndev, 128), F32),
            pltpu.VMEM((ndev, 128), jnp.int32),
            pltpu.SMEM((ndev, 128), jnp.int32),
            pltpu.VMEM((ndev, rows, rank), BF16),
            pltpu.VMEM((ndev, rows, rank), BF16),
            pltpu.VMEM((3 * nl, 3, 112, leaf), BF16),
            pltpu.VMEM((3 * nl, 48, leaf), BF16),
            pltpu.VMEM((3 * nl, leaf, 16), F32),
            pltpu.VMEM((2, 4, leaf, leaf), BF16),
            pltpu.VMEM((3, 16, width), F32),
            pltpu.VMEM((per_row * 16, rank), F32),
            pltpu.VMEM((per_row, 16, rank), BF16),
            pltpu.SemaphoreType.DMA((10,)),
            pltpu.SemaphoreType.DMA((2,)),
            pltpu.SemaphoreType.DMA((2,)),
            pltpu.SemaphoreType.DMA((ndev,)),
            pltpu.SemaphoreType.DMA((ndev,)),
        ],
        compiler_params=pltpu.CompilerParams(
            collective_id=0, has_side_effects=True, vmem_limit_bytes=50 * 1024 * 1024
        ),
    )(pack, jnp.transpose(basis, (0, 2, 1, 3)), up_leaf, up_mid, up_top,
      couplings.reshape(per_row * fan, rank, rank), far_dest, far_target, near_src)
    return jnp.transpose(out[:, :cases], (1, 0, 2))


def solution(mesh):
    every = ("groups", "clus", "sub")
    return jax.shard_map(
        body,
        mesh=mesh,
        in_specs=(
            P(None, None, every),
            P(None, every),
            P(every, None, None, None),
            P(every, None, None),
            P(every, None, None),
            P(every, None, None),
            P(every, None, None, None),
            P(every, None),
            P(every, None),
            P(every, None),
        ),
        out_specs=P(None, None, every),
        check_vma=False,
    )
```
